1024 devices in a mesh: wide: 128 (over y, z_lo, core), narrow: 8 (over x, z_hi).
Axes of the slice: x: 4, y: 4, z: 32 (z_hi: 2, z_lo: 16; z = z_hi * 16 + z_lo), core: 2. Of those that a mesh axis runs over, the one named last changes fastest.
Arguments:
- features: bfloat16 [262144, 128], P(('wide', 'narrow')), may hold values from -6 to 6
- w_self: bfloat16 [128, 256], replicated, may hold values from -0.5 to 0.5
- w_neigh: bfloat16 [128, 256], replicated, may hold values from -3 to 3
- cotangent: bfloat16 [262144, 256], P(('wide', 'narrow')), may hold values from -6 to 6
- tile_src: int32 [2048, 20], P(('wide', 'narrow')), may hold values from 0 to 79, as said below
- tile_live: int32 [2048], P(('wide', 'narrow')), may hold values from 2 to 20, as said below
- tile_mask: int32 [2048, 20, 128, 128], P(('wide', 'narrow')), may hold values 0 or 1
Outputs:
- output: bfloat16 [262144, 256], P(('wide', 'narrow'))
- grad_self: float32 [128, 256], replicated
- grad_neigh: float32 [128, 256], replicated
- grad_input: bfloat16 [262144, 128], P(('wide', 'narrow'))
The draws below stay inside these ranges and needn't reach their ends.
Inputs may be any that keep to these rules, and one draw needn't show every extreme that they name: `tile_src`: the 20 entries of a row are different. Entry s names tile s % 16 of the row block that lies s // 16 - 2 places further along the closed order of row blocks. Slots from tile_live onward are unused whatever their mask holds; some row tile uses all 20 slots.
All inputs are finite; a program needn't handle non-finite values. No bound on the sum of `tile_mask` on one device may be relied on, other than what follows from the above.
Results may differ from the reference program's by a relative error of at most 0.0057.
Values may be sent and summed in bfloat16 or wider, within the bound.
A program may use at most 32 MiB of HBM per device.

```python
import math
import jax
import jax.numpy as jnp
from jax import lax

F = 128
HID = 256
TILE = 128
CAP = 20
REACH = 2
NODES = 262144
BLOCK_TILES = 16
WINDOW_TILES = 80
N_WIDE = 128


def draw_tile_src(key, part):
    key = jax.random.fold_in(key, 11)
    tile_keys = jax.random.split(key, NODES // TILE)
    return jax.vmap(lambda one_key: jax.random.permutation(one_key, WINDOW_TILES)[:CAP])(tile_keys).astype(jnp.int32)


def draw_tile_live(key, part):
    key = jax.random.fold_in(key, 12)
    first_key, second_key, third_key = jax.random.split(key, 3)
    tile_count = NODES // TILE
    first = jax.random.randint(first_key, (tile_count,), 2, CAP + 1)
    second = jax.random.randint(second_key, (tile_count,), 2, CAP + 1)
    fullest = jax.random.randint(third_key, (), 0, tile_count)
    live_count = jnp.minimum(first, second)
    return jnp.where(jnp.arange(tile_count) == fullest, CAP, live_count).astype(jnp.int32)


def touch_ends(result, rng, smallest, high):
    extent = result.shape
    spot = [jax.random.randint(jax.random.fold_in(rng, axis), (), 0, extent[axis]) for axis in range(len(extent))]
    result = result.at[tuple(spot)].set(smallest)
    longest = extent.index(max(extent))
    spot[longest] = (spot[longest] + 1) % extent[longest]
    return result.at[tuple(spot)].set(high)


def shard_levels(own_key, extent, shards, low, top_value):
    loudness, own = 1.0, jax.random.fold_in(own_key, 6)
    for position, parts in shards:
        steps = jnp.exp(jax.random.uniform(jax.random.fold_in(own, position), (parts,), jnp.float32, low / len(shards), top_value / len(shards)))
        loudness = loudness * jnp.repeat(steps, extent[position] // parts).reshape([-1 if axis == position else 1 for axis in range(len(extent))])
    return loudness


def normal_values(key, dims, spread, most, cuts=(), kind=jnp.bfloat16):
    drawn = spread * jax.random.normal(key, dims, jnp.float32)
    if cuts:
        drawn = drawn * shard_levels(key, dims, cuts, -0.22, 0.18)
    return jnp.clip(drawn, -most, most).astype(kind)


def setup_inputs(seed: int = 0) -> dict:
    key_list = jax.random.split(jax.random.key(seed), 8)
    return {
        "features": normal_values(key_list[0], (NODES, F), 1.0, 6.0, ((0, 1024),)),
        "w_self": normal_values(key_list[1], (F, HID), F ** -0.5, 0.5),
        "w_neigh": normal_values(key_list[2], (F, HID), (F // 32) ** -0.5, 3.0),
        "cotangent": normal_values(key_list[3], (NODES, HID), 1.0, 6.0, ((0, 1024),)),
        "tile_src": draw_tile_src(jax.random.fold_in(key_list[7], 71), 0),
        "tile_live": draw_tile_live(jax.random.fold_in(key_list[7], 71), 0),
        "tile_mask": touch_ends((jax.random.randint(key_list[6], (NODES // TILE, CAP, TILE, TILE), 0, TILE // 4) < 1).astype(jnp.int32), jax.random.fold_in(key_list[6], 1), 0, 1),
    }


def reference(features, w_self, w_neigh, cotangent, tile_src, tile_live, tile_mask):
    width = features.shape[1]
    tile_count = NODES // TILE
    feature_tiles = features.reshape(tile_count, TILE, width)
    home_block = (jnp.arange(tile_count, dtype=jnp.int32) // BLOCK_TILES)[:, None]
    offset = tile_src // BLOCK_TILES - REACH
    source = ((home_block + offset) % N_WIDE * BLOCK_TILES + tile_src % BLOCK_TILES).astype(jnp.int32)
    live_slots = jnp.arange(CAP, dtype=jnp.int32)[None, :] < tile_live[:, None]

    def gather_tile(inputs):
        source_row, live_row, mask_row = inputs
        adjacency = jnp.where(live_row[:, None, None], mask_row, 0).astype(jnp.float32)
        picked = feature_tiles[source_row].astype(jnp.float32)
        summed = jnp.einsum('cij,cjf->if', adjacency, picked)
        return (summed, lax.optimization_barrier(jnp.sum(adjacency, axis=(0, 2))))
    summed, degree = lax.map(gather_tile, (source, live_slots, tile_mask))
    scaling = 1.0 / (1.0 + degree.reshape(NODES))
    mean_rows = (summed.reshape(NODES, width) * scaling[:, None]).astype(jnp.bfloat16)
    preact = jnp.dot(features, w_self, preferred_element_type=jnp.float32) + jnp.dot(mean_rows, w_neigh, preferred_element_type=jnp.float32)
    output = jax.nn.silu(preact).astype(jnp.bfloat16)
    sigmoid_pre = jax.nn.sigmoid(preact)
    grad_pre = (cotangent.astype(jnp.float32) * sigmoid_pre * (1.0 + preact * (1.0 - sigmoid_pre))).astype(jnp.bfloat16)
    factor = 1.0 / math.sqrt(NODES)
    grad_self = jnp.dot(features.T, grad_pre, preferred_element_type=jnp.float32) * factor
    grad_neigh = jnp.dot(mean_rows.T, grad_pre, preferred_element_type=jnp.float32) * factor
    pulled = (jnp.dot(grad_pre, w_neigh.T, preferred_element_type=jnp.float32) * scaling[:, None]).astype(jnp.bfloat16)
    local_term = jnp.dot(grad_pre, w_self.T, preferred_element_type=jnp.float32)
    pulled_tiles = pulled.reshape(tile_count, TILE, width)

    def scatter_tile(accumulator, inputs):
        source_row, live_row, mask_row, pulled_tile = inputs
        adjacency = jnp.where(live_row[:, None, None], mask_row, 0).astype(jnp.float32)
        terms = jnp.einsum('cij,if->cjf', adjacency, pulled_tile.astype(jnp.float32))
        return (accumulator.at[source_row].add(terms), None)
    accumulator, unused = lax.scan(scatter_tile, jnp.zeros((tile_count, TILE, width), jnp.float32), (source, live_slots, tile_mask, pulled_tiles))
    grad_input = (local_term + accumulator.reshape(NODES, width)).astype(jnp.bfloat16)
    return (output, grad_self, grad_neigh, grad_input)
```

```python
import functools
import math

import jax
import jax.numpy as jnp
from jax import lax
from jax.experimental import pallas as pl
from jax.experimental.pallas import tpu as pltpu
from jax.sharding import PartitionSpec as P

REACH = 2
WINDOW = 2 * REACH + 1
XS, YS, ZS, CORES = 4, 4, 32, 2
Z_LO = 16
TILE = 128
SHARD = 2 * TILE
BLOCK_TILES = 16
WINDOW_TILES = WINDOW * BLOCK_TILES
SHARDS = WINDOW_TILES // 2
TRANSFERS = 128
GREETINGS = 17
F32 = jnp.float32
BF16 = jnp.bfloat16


def device_of(x, y, z, core):
    return ((y * Z_LO + z % Z_LO) * CORES + core, x * 2 + z // Z_LO)


def kernel(
    slots,
    features_hbm,
    w_self_hbm,
    w_neigh_hbm,
    cotangent_hbm,
    tile_src_hbm,
    tile_live_hbm,
    tile_mask_hbm,
    output,
    grad_self,
    grad_neigh,
    grad_input,
    w_self,
    w_neigh,
    cotangent,
    tile_src,
    tile_live,
    mask_in,
    mask_rows,
    mask_cols,
    slot_vec,
    slot_of,
    adj,
    adj_t,
    win,
    summed,
    degree,
    pre_self,
    mean_rows,
    pulled,
    local_term,
    core_out,
    core_in,
    x_out,
    x_in,
    own_part,
    z_out,
    z_in,
    own_total,
    far_out,
    far_in,
    grads,
    grads_core,
    grads_y,
    grads_x,
    grads_pair,
    grads_near,
    grads_far,
    grads_all,
    send_sem,
    recv_sem,
    load_sem,
    slot_sem,
):
    wide, narrow = lax.axis_index("wide"), lax.axis_index("narrow")
    core = wide % 2
    z_lo = (wide // 2) % Z_LO
    y = wide // (2 * Z_LO)
    x = narrow // 2
    h = narrow % 2
    z = h * Z_LO + z_lo

    other_core = device_of(x, y, z, 1 - core)
    xs = [(x + step) % XS for step in (1, 3, 2)]
    ys = [(y + step) % YS for step in (1, 3, 2)]
    from_xs = [xs[1], xs[0], xs[2]]
    x_devices = [device_of(to, y, z, core) for to in xs]
    y_devices = [device_of(x, to, z, core) for to in ys]
    far = device_of(x, y, (z + 16) % ZS, core)
    prev_y = jnp.where(z_lo == 0, (y + YS - 1) % YS, y)
    next_y = jnp.where(z_lo == Z_LO - 1, (y + 1) % YS, y)
    prev_z, next_z = (z + ZS - 1) % ZS, (z + 1) % ZS
    prev = device_of(x, prev_y, prev_z, core)
    next_ = device_of(x, next_y, next_z, core)
    pair_z = z + 1 - 2 * (z % 2)
    pair = device_of(x, y, pair_z, core)
    near_slot = (z // 2) % 4
    near_devices = [
        device_of(x, y, (z // 8) * 8 + ((near_slot + step) % 4) * 2 + z % 2, core) for step in (1, 3, 2)
    ]
    far_slot = z // 8
    far_devices = [device_of(x, y, ((far_slot + step) % 4) * 8 + z % 8, core) for step in (1, 3, 2)]
    h_prev, h_next = prev_z // Z_LO, next_z // Z_LO

    barrier = pltpu.get_barrier_semaphore()
    greeted = [other_core, *x_devices, *y_devices, far, prev, next_, pair, *near_devices, *far_devices]
    for device in greeted:
        pl.semaphore_signal(barrier, inc=1, device_id=device, device_id_type=pl.DeviceIdType.MESH)

    sent = []

    def send(source, target, device):
        number = len(sent)
        copy = pltpu.make_async_remote_copy(
            src_ref=source,
            dst_ref=target,
            send_sem=send_sem.at[number],
            recv_sem=recv_sem.at[number],
            device_id=device,
            device_id_type=pl.DeviceIdType.MESH,
        )
        copy.start()
        sent.append(copy)
        return copy

    loads = [
        pltpu.make_async_copy(source, target, load_sem.at[number])
        for number, (source, target) in enumerate(
            (
                (tile_src_hbm, tile_src),
                (tile_live_hbm, tile_live),
                (features_hbm, win.at[2, x, h]),
                (w_self_hbm, w_self),
                (tile_mask_hbm, mask_in),
                (w_neigh_hbm, w_neigh),
                (cotangent_hbm, cotangent),
            )
        )
    ]
    for load in loads:
        load.start()
    load_src, load_live, load_features, load_self, load_mask, load_neigh, load_cotangent = loads

    load_src.wait()
    load_live.wait()
    window_tile = lax.broadcasted_iota(jnp.int32, (8, TILE), 1)
    for d in range(2):

        def find(c, found, d=d):
            source = jnp.where(c < tile_live[d], tile_src[d, c], -1)
            return jnp.where(window_tile == source, c, found)

        slot_vec[d * 8 : d * 8 + 8, :] = lax.fori_loop(0, slots, find, jnp.full((8, TILE), slots, jnp.int32))
    load_slots = pltpu.make_async_copy(slot_vec, slot_of, slot_sem)
    load_slots.start()

    load_features.wait()
    load_self.wait()
    pre_self[...] = jnp.dot(win[2, x, h], w_self[...], preferred_element_type=F32)
    core_in[0, 2 * core] = jnp.zeros((XS, SHARD, TILE), BF16)
    core_in[1, 2 * core] = jnp.zeros((XS, SHARD, TILE), BF16)
    for d in range(2):
        mask_rows[d * (slots + 1) + slots] = jnp.zeros((TILE, TILE), BF16)
        mask_cols[d * (slots + 1) + slots] = jnp.zeros((TILE, TILE), BF16)

    load_mask.wait()
    for d in range(2):

        @pl.loop(0, slots)
        def _(c, d=d):
            tile = mask_in[d, c].astype(F32)
            mask_rows[d * (slots + 1) + c] = tile.astype(BF16)
            mask_cols[d * (slots + 1) + c] = tile.T.astype(BF16)

    pl.semaphore_wait(barrier, GREETINGS)

    side_p = 4 - 4 * core
    side_h = jnp.where(core == 0, h_next, h_prev)

    def spread(hi, first):
        own = win.at[2, x, hi]
        to_far = send(own, own, far) if first else None
        to_next = send(own, win.at[0, x, hi], next_)
        to_prev = send(own, win.at[4, x, hi], prev)
        over_x = [send(own, own, device) for device in x_devices]
        to_core = send(own, win.at[1 + 2 * core, x, hi], other_core)
        return to_far, to_next, to_prev, over_x, to_core

    def spread_sides(flip, to_next, to_prev):
        hi_prev, hi_next = (h_prev, h_next) if flip == 0 else (1 - h_prev, 1 - h_next)
        side = side_h if flip == 0 else 1 - side_h
        to_next.wait_recv()
        from_prev = win.at[0, x, hi_prev]
        over_prev = [send(from_prev, from_prev, device) for device in x_devices]
        to_prev.wait_recv()
        from_next = win.at[4, x, hi_next]
        over_next = [send(from_next, from_next, device) for device in x_devices]
        to_core = send(win.at[side_p, x, side], win.at[3 - 2 * core, x, side], other_core)
        return over_prev, over_next, to_core

    def spread_cores(flip, over_x, over_prev, over_next):
        hi = h if flip == 0 else 1 - h
        side = side_h if flip == 0 else 1 - side_h
        copies = []
        for j in range(3):
            over_x[j].wait_recv()
            copies.append(send(win.at[2, from_xs[j], hi], win.at[1 + 2 * core, from_xs[j], hi], other_core))
        for j in range(3):
            over_prev[j].wait_recv()
            over_next[j].wait_recv()
            copies.append(
                send(
                    win.at[side_p, from_xs[j], side], win.at[3 - 2 * core, from_xs[j], side], other_core
                )
            )
        return copies

    def sides(flip):
        parts = [h_prev, jnp.where(core == 0, h_prev, h), h, jnp.where(core == 0, h, h_next), h_next]
        return parts if flip == 0 else [1 - part for part in parts]

    to_far, to_next, to_prev, over_x, to_core = spread(h, True)

    load_slots.wait()
    degree[...] = jnp.zeros((SHARD, TILE), F32)

    @pl.loop(0, SHARDS)
    def _(s):
        for t in range(2):
            for d in range(2):
                index = d * (slots + 1) + jnp.clip(slot_of[8 * d, 2 * s + t], 0, slots)
                adj[s, pl.ds(d * TILE, TILE), pl.ds(t * TILE, TILE)] = mask_rows[index]
                adj_t[s, pl.ds(t * TILE, TILE), pl.ds(d * TILE, TILE)] = mask_cols[index]
        degree[...] += jnp.dot(adj[s], jnp.ones((SHARD, TILE), BF16), preferred_element_type=F32)

    over_prev, over_next, side_core = spread_sides(0, to_next, to_prev)
    cores_0 = spread_cores(0, over_x, over_prev, over_next)

    summed[...] = jnp.zeros((SHARD, TILE), F32)

    def aggregate(blocks, parts):
        for p in blocks:

            @pl.loop(0, XS)
            def _(xo, p=p):
                summed[...] += jnp.dot(
                    adj[(p * XS + xo) * 2 + parts[p]], win[p, xo, parts[p]], preferred_element_type=F32
                )

    parts_0, parts_1 = sides(0), sides(1)
    aggregate((0, 2, 4), parts_0)

    to_far.wait_recv()
    _, to_next_1, to_prev_1, over_x_1, to_core_1 = spread(1 - h, False)
    to_core.wait_recv()
    side_core.wait_recv()
    for copy in cores_0:
        copy.wait_recv()
    aggregate((1, 3), parts_0)
    over_prev_1, over_next_1, side_core_1 = spread_sides(1, to_next_1, to_prev_1)
    cores_1 = spread_cores(1, over_x_1, over_prev_1, over_next_1)
    aggregate((0, 2, 4), parts_1)
    to_core_1.wait_recv()
    side_core_1.wait_recv()
    for copy in cores_1:
        copy.wait_recv()
    aggregate((1, 3), parts_1)

    load_neigh.wait()
    load_cotangent.wait()
    scaling = 1.0 / (1.0 + degree[...])
    mean_rows[...] = (summed[...] * scaling).astype(BF16)
    preact = pre_self[...] + jnp.dot(mean_rows[...], w_neigh[...], preferred_element_type=F32)
    sigmoid = jax.nn.sigmoid(preact)
    output[...] = (preact * sigmoid).astype(BF16)
    grad_pre = (cotangent[...].astype(F32) * sigmoid * (1.0 + preact * (1.0 - sigmoid))).astype(BF16)
    rows_first = (((0,), (0,)), ((), ()))
    hidden_last = (((1,), (1,)), ((), ()))
    grads[0] = lax.dot_general(win[2, x, h], grad_pre, rows_first, preferred_element_type=F32)
    grads[1] = lax.dot_general(mean_rows[...], grad_pre, rows_first, preferred_element_type=F32)
    core_grads = send(grads.at[1 - core], grads_core, other_core)
    pulled[...] = (
        lax.dot_general(grad_pre, w_neigh[...], hidden_last, preferred_element_type=F32) * scaling
    ).astype(BF16)
    local_term[...] = lax.dot_general(grad_pre, w_self[...], hidden_last, preferred_element_type=F32)

    def to_cores(phase, parts):
        copies = []
        for i in range(2):
            p = 2 * i + 1

            @pl.loop(0, XS)
            def _(xo, i=i, p=p):
                core_out[phase, i, xo] = jnp.dot(
                    adj_t[(p * XS + xo) * 2 + parts[p]], pulled[...], preferred_element_type=F32
                ).astype(BF16)

            copies.append(send(core_out.at[phase, i], core_in.at[phase, i + core], other_core))
        return copies

    def over_x_back(phase, parts, blocks):
        copies = []
        for q in blocks:
            p = 2 * q

            @pl.loop(0, 3)
            def _(j, q=q, p=p):
                step = jnp.where(j == 0, 1, jnp.where(j == 1, 3, 2))
                xo = (x + step) % XS
                x_out[phase, q, j] = (
                    jnp.dot(
                        adj_t[(p * XS + xo) * 2 + parts[p]], pulled[...], preferred_element_type=F32
                    )
                    + core_in[phase, q, xo].astype(F32)
                ).astype(BF16)

            for j in range(3):
                copies.append(send(x_out.at[phase, q, j], x_in.at[phase, q, j], x_devices[j]))
        for q in blocks:
            p = 2 * q
            own_part[phase, q] = jnp.dot(
                adj_t[(p * XS + x) * 2 + parts[p]], pulled[...], preferred_element_type=F32
            ) + core_in[phase, q, x].astype(F32)
        return copies

    def x_sum(phase, q):
        total = own_part[phase, q]
        for j in range(3):
            total = total + x_in[phase, q, j].astype(F32)
        return total

    def to_sides(phase, copies):
        for copy in copies:
            copy.wait_recv()
        z_out[phase, 0] = x_sum(phase, 0).astype(BF16)
        to_prev = send(z_out.at[phase, 0], z_in.at[phase, 1], prev)
        z_out[phase, 1] = x_sum(phase, 2).astype(BF16)
        to_next = send(z_out.at[phase, 1], z_in.at[phase, 0], next_)
        return to_prev, to_next

    cores_back_1 = to_cores(1, parts_1)
    cores_back_0 = to_cores(0, parts_0)
    core_grads.wait_recv()
    grads[core] = grads[core] + grads_core[...]
    y_rows = TILE // YS
    x_rows = y_rows // XS
    y_grads = [
        send(grads.at[core, pl.ds(ys[j] * y_rows, y_rows)], grads_y.at[j], y_devices[j]) for j in range(3)
    ]
    for copy in cores_back_1:
        copy.wait_recv()
    x_sides_1 = over_x_back(1, parts_1, (0, 2))
    x_own_1 = over_x_back(1, parts_1, (1,))
    for copy in y_grads:
        copy.wait_recv()
    own_rows = pl.ds(y * y_rows, y_rows)
    grads_all[0, :y_rows] = grads[core, own_rows] + grads_y[0] + grads_y[1] + grads_y[2]
    x_grads = [
        send(grads_all.at[0, pl.ds(xs[j] * x_rows, x_rows)], grads_x.at[j], x_devices[j]) for j in range(3)
    ]
    for copy in cores_back_0:
        copy.wait_recv()
    x_sides_0 = over_x_back(0, parts_0, (0, 2))
    x_own_0 = over_x_back(0, parts_0, (1,))
    for copy in x_grads:
        copy.wait_recv()
    part = grads_all[0, pl.ds(x * x_rows, x_rows)] + grads_x[0] + grads_x[1] + grads_x[2]
    grads_pair[0] = part[:, :TILE]
    grads_pair[1] = part[:, TILE:]
    parity = z % 2
    pair_grads = send(grads_pair.at[1 - parity], grads_pair.at[2], pair)
    pair_grads.wait_recv()
    grads_near[near_slot] = grads_pair[parity] + grads_pair[2]
    near_grads = [send(grads_near.at[near_slot], grads_near.at[near_slot], device) for device in near_devices]
    sides_1 = to_sides(1, x_sides_1)
    for copy in near_grads:
        copy.wait_recv()
    grads_far[far_slot] = grads_near[0] + grads_near[1] + grads_near[2] + grads_near[3]
    far_grads = [send(grads_far.at[far_slot], grads_far.at[far_slot], device) for device in far_devices]
    for copy in (*x_own_1, *sides_1):
        copy.wait_recv()
    far_out[...] = (x_sum(1, 1) + z_in[1, 0].astype(F32) + z_in[1, 1].astype(F32)).astype(BF16)
    to_far_back = send(far_out, far_in, far)
    sides_0 = to_sides(0, x_sides_0)
    for copy in (*x_own_0, *sides_0):
        copy.wait_recv()
    own_total[...] = (
        local_term[...] + x_sum(0, 1) + z_in[0, 0].astype(F32) + z_in[0, 1].astype(F32)
    )
    for copy in far_grads:
        copy.wait_recv()
    factor = 1.0 / math.sqrt(SHARD * lax.axis_size("wide") * lax.axis_size("narrow"))
    total = (grads_far[0] + grads_far[1] + grads_far[2] + grads_far[3]) * factor
    row = y * y_rows + x * x_rows
    piece = grads_all.at[1 + core, pl.ds(row, x_rows), pl.ds(pl.multiple_of(parity * TILE, TILE), TILE)]
    piece[...] = total
    send(piece, piece, pair).wait_recv()
    piece = grads_all.at[1 + core, pl.ds(row, x_rows)]
    for copy in [send(piece, piece, device) for device in x_devices]:
        copy.wait_recv()
    piece = grads_all.at[1 + core, pl.ds(y * y_rows, y_rows)]
    for copy in [send(piece, piece, device) for device in y_devices]:
        copy.wait_recv()
    piece = grads_all.at[1 + core]
    send(piece, piece, other_core).wait_recv()
    grad_self[...] = grads_all[1]
    grad_neigh[...] = grads_all[2]
    to_far_back.wait_recv()
    grad_input[...] = (own_total[...] + far_in[...].astype(F32)).astype(BF16)
    for copy in sent:
        copy.wait_send()


def body(features, w_self, w_neigh, cotangent, tile_src, tile_live, tile_mask):
    rows, width = features.shape
    hidden = w_self.shape[1]
    slots = tile_src.shape[1]
    vmem = pl.BlockSpec(memory_space=pltpu.VMEM)
    hbm = pl.BlockSpec(memory_space=pl.ANY)
    return pl.pallas_call(
        functools.partial(kernel, slots),
        out_shape=(
            jax.ShapeDtypeStruct((rows, hidden), BF16),
            jax.ShapeDtypeStruct((width, hidden), F32),
            jax.ShapeDtypeStruct((width, hidden), F32),
            jax.ShapeDtypeStruct((rows, width), BF16),
        ),
        in_specs=[hbm] * 7,
        out_specs=[vmem] * 4,
        scratch_shapes=[
            pltpu.VMEM((width, hidden), BF16),
            pltpu.VMEM((width, hidden), BF16),
            pltpu.VMEM((rows, hidden), BF16),
            pltpu.SMEM(tile_src.shape, jnp.int32),
            pltpu.SMEM(tile_live.shape, jnp.int32),
            pltpu.VMEM((2, slots, TILE, TILE), jnp.int32),
            pltpu.VMEM((2 * (slots + 1), TILE, TILE), BF16),
            pltpu.VMEM((2 * (slots + 1), TILE, TILE), BF16),
            pltpu.VMEM((16, TILE), jnp.int32),
            pltpu.SMEM((16, TILE), jnp.int32),
            pltpu.VMEM((SHARDS, SHARD, SHARD), BF16),
            pltpu.VMEM((SHARDS, SHARD, SHARD), BF16),
            pltpu.VMEM((WINDOW, XS, 2, SHARD, TILE), BF16),
            pltpu.VMEM((SHARD, TILE), F32),
            pltpu.VMEM((SHARD, TILE), F32),
            pltpu.VMEM((SHARD, hidden), F32),
            pltpu.VMEM((SHARD, TILE), BF16),
            pltpu.VMEM((SHARD, TILE), BF16),
            pltpu.VMEM((SHARD, TILE), F32),
            pltpu.VMEM((2, 2, XS, SHARD, TILE), BF16),
            pltpu.VMEM((2, 3, XS, SHARD, TILE), BF16),
            pltpu.VMEM((2, 3, 3, SHARD, TILE), BF16),
            pltpu.VMEM((2, 3, 3, SHARD, TILE), BF16),
            pltpu.VMEM((2, 3, SHARD, TILE), F32),
            pltpu.VMEM((2, 2, SHARD, TILE), BF16),
            pltpu.VMEM((2, 2, SHARD, TILE), BF16),
            pltpu.VMEM((SHARD, TILE), F32),
            pltpu.VMEM((SHARD, TILE), BF16),
            pltpu.VMEM((SHARD, TILE), BF16),
            pltpu.VMEM((2, width, hidden), F32),
            pltpu.VMEM((width, hidden), F32),
            pltpu.VMEM((3, width // YS, hidden), F32),
            pltpu.VMEM((3, width // YS // XS, hidden), F32),
            pltpu.VMEM((3, width // YS // XS, TILE), F32),
            pltpu.VMEM((4, width // YS // XS, TILE), F32),
            pltpu.VMEM((4, width // YS // XS, TILE), F32),
            pltpu.VMEM((3, width, hidden), F32),
            pltpu.SemaphoreType.DMA((TRANSFERS,)),
            pltpu.SemaphoreType.DMA((TRANSFERS,)),
            pltpu.SemaphoreType.DMA((7,)),
            pltpu.SemaphoreType.DMA,
        ],
        compiler_params=pltpu.CompilerParams(
            collective_id=1, has_side_effects=True, vmem_limit_bytes=62 * 1024 * 1024
        ),
    )(features, w_self, w_neigh, cotangent, tile_src, tile_live, tile_mask)


def solution(mesh):
    return jax.shard_map(
        body,
        mesh=mesh,
        in_specs=(
            P(("wide", "narrow"), None),
            P(),
            P(),
            P(("wide", "narrow"), None),
            P(("wide", "narrow"), None),
            P(("wide", "narrow")),
            P(("wide", "narrow"), None, None, None),
        ),
        out_specs=(P(("wide", "narrow"), None), P(), P(), P(("wide", "narrow"), None)),
        check_vma=False,
    )
```

```python
import functools
import math

import jax
import jax.numpy as jnp
from jax import lax
from jax.experimental import pallas as pl
from jax.experimental.pallas import tpu as pltpu
from jax.sharding import PartitionSpec as P

REACH = 2
WINDOW = 2 * REACH + 1
XS, YS, ZS, CORES = 4, 4, 32, 2
Z_LO = 16
TILE = 128
SHARD = 2 * TILE
BLOCK_TILES = 16
WINDOW_TILES = WINDOW * BLOCK_TILES
SHARDS = WINDOW_TILES // 2
PLANE = XS * YS
NEAR, FAR = 8, 4
TRANSFERS = 192
F32 = jnp.float32
BF16 = jnp.bfloat16


def device_of(x, y, z, core):
    return ((y * Z_LO + z % Z_LO) * CORES + core, x * 2 + z // Z_LO)


def kernel(
    slots,
    features_hbm,
    w_self_hbm,
    w_neigh_hbm,
    cotangent_hbm,
    tile_src_hbm,
    tile_live_hbm,
    tile_mask_hbm,
    output,
    grad_self,
    grad_neigh,
    grad_input,
    w_self,
    w_neigh,
    cotangent,
    tile_src,
    tile_live,
    mask_in,
    mask_rows,
    mask_cols,
    slot_vec,
    slot_of,
    adj,
    adj_t,
    win,
    summed,
    degree,
    pre_self,
    mean_rows,
    pulled,
    local_term,
    core_out,
    core_in,
    x_out,
    x_in,
    own_part,
    zx_out,
    zx_in,
    z_out,
    z_in,
    own_total,
    far_out,
    far_in,
    grads,
    grads_core,
    grads_plane,
    grads_near,
    grads_far,
    grads_all,
    send_sem,
    recv_sem,
    load_sem,
    slot_sem,
):
    wide, narrow = lax.axis_index("wide"), lax.axis_index("narrow")
    core = wide % 2
    z_lo = (wide // 2) % Z_LO
    y = wide // (2 * Z_LO)
    x = narrow // 2
    h = narrow % 2
    z = h * Z_LO + z_lo

    other_core = device_of(x, y, z, 1 - core)
    xs = [(x + step) % XS for step in (1, 3, 2)]
    from_xs = [xs[1], xs[0], xs[2]]
    x_devices = [device_of(to, y, z, core) for to in xs]
    far = device_of(x, y, (z + 16) % ZS, core)
    prev_y = jnp.where(z_lo == 0, (y + YS - 1) % YS, y)
    next_y = jnp.where(z_lo == Z_LO - 1, (y + 1) % YS, y)
    prev_z, next_z = (z + ZS - 1) % ZS, (z + 1) % ZS
    prev = device_of(x, prev_y, prev_z, core)
    next_ = device_of(x, next_y, next_z, core)
    place = y * XS + x
    places = [(place + step) % PLANE for step in range(1, PLANE)]
    plane_devices = [device_of(to % XS, to // XS, z, core) for to in places]
    near_slot, far_slot = z % NEAR, z // NEAR
    near_devices = [
        device_of(x, y, far_slot * NEAR + (near_slot + step) % NEAR, core) for step in range(1, NEAR)
    ]
    far_devices = [
        device_of(x, y, ((far_slot + step) % FAR) * NEAR + near_slot, core) for step in range(1, FAR)
    ]
    h_prev, h_next = prev_z // Z_LO, next_z // Z_LO

    barrier = pltpu.get_barrier_semaphore()
    greeted = [other_core, *plane_devices, prev, next_, *near_devices, *far_devices]
    for device in greeted:
        pl.semaphore_signal(barrier, inc=1, device_id=device, device_id_type=pl.DeviceIdType.MESH)

    sent = []

    def send(source, target, device):
        number = len(sent)
        copy = pltpu.make_async_remote_copy(
            src_ref=source,
            dst_ref=target,
            send_sem=send_sem.at[number],
            recv_sem=recv_sem.at[number],
            device_id=device,
            device_id_type=pl.DeviceIdType.MESH,
        )
        copy.start()
        sent.append(copy)
        return copy

    loads = [
        pltpu.make_async_copy(source, target, load_sem.at[number])
        for number, (source, target) in enumerate(
            (
                (tile_src_hbm, tile_src),
                (tile_live_hbm, tile_live),
                (features_hbm, win.at[2, x, h]),
                (w_self_hbm, w_self),
                (tile_mask_hbm, mask_in),
                (w_neigh_hbm, w_neigh),
                (cotangent_hbm, cotangent),
            )
        )
    ]
    for load in loads:
        load.start()
    load_src, load_live, load_features, load_self, load_mask, load_neigh, load_cotangent = loads

    load_src.wait()
    load_live.wait()
    window_tile = lax.broadcasted_iota(jnp.int32, (8, TILE), 1)
    for d in range(2):

        def find(c, found, d=d):
            source = jnp.where(c < tile_live[d], tile_src[d, c], -1)
            return jnp.where(window_tile == source, c, found)

        slot_vec[d * 8 : d * 8 + 8, :] = lax.fori_loop(0, slots, find, jnp.full((8, TILE), slots, jnp.int32))
    load_slots = pltpu.make_async_copy(slot_vec, slot_of, slot_sem)
    load_slots.start()

    load_features.wait()
    load_self.wait()
    pre_self[...] = jnp.dot(win[2, x, h], w_self[...], preferred_element_type=F32)
    core_in[0, 2 * core] = jnp.zeros((XS, SHARD, TILE), BF16)
    core_in[1, 2 * core] = jnp.zeros((XS, SHARD, TILE), BF16)
    for d in range(2):
        mask_rows[d * (slots + 1) + slots] = jnp.zeros((TILE, TILE), BF16)
        mask_cols[d * (slots + 1) + slots] = jnp.zeros((TILE, TILE), BF16)

    load_mask.wait()
    degree[...] = jnp.zeros((SHARD, TILE), F32)
    for d in range(2):

        @pl.loop(0, slots)
        def _(c, d=d):
            used = jnp.where(c < tile_live[d], 1, 0)
            degree[pl.ds(d * TILE, TILE)] += (mask_in[d, c] * used).astype(F32)
            tile = mask_in[d, c].astype(F32)
            mask_rows[d * (slots + 1) + c] = tile.astype(BF16)
            mask_cols[d * (slots + 1) + c] = tile.T.astype(BF16)

    degree[...] = jnp.dot(degree[...].astype(BF16), jnp.ones((TILE, TILE), BF16), preferred_element_type=F32)

    pl.semaphore_wait(barrier, len(greeted))

    side_p = 4 - 4 * core
    side_h = jnp.where(core == 0, h_next, h_prev)
    shard = pl.ds(0, SHARD)
    tiles = [pl.ds(t * TILE, TILE) for t in range(2)]

    def spread(flip, rows):
        hi = h if flip == 0 else 1 - h
        own = win.at[2, x, hi, rows]
        to_next = send(own, win.at[0, x, hi, rows], next_)
        to_prev = send(own, win.at[4, x, hi, rows], prev)
        over_x = [send(own, own, x_devices[j]) for j in (2, 0, 1)]
        over_x = [over_x[1], over_x[2], over_x[0]]
        to_core = send(own, win.at[1 + 2 * core, x, hi, rows], other_core)
        return to_next, to_prev, over_x, to_core

    def spread_sides(flip, rows, to_next, to_prev):
        hi_prev, hi_next = (h_prev, h_next) if flip == 0 else (1 - h_prev, 1 - h_next)
        side = side_h if flip == 0 else 1 - side_h
        to_next.wait_recv()
        from_prev = win.at[0, x, hi_prev, rows]
        over_prev = [send(from_prev, from_prev, device) for device in x_devices[:2]]
        to_prev.wait_recv()
        from_next = win.at[4, x, hi_next, rows]
        over_next = [send(from_next, from_next, device) for device in x_devices[:2]]
        to_core = send(win.at[side_p, x, side, rows], win.at[3 - 2 * core, x, side, rows], other_core)
        return over_prev, over_next, to_core

    def spread_cores(flip, rows, over_x, over_prev, over_next):
        hi = h if flip == 0 else 1 - h
        side = side_h if flip == 0 else 1 - side_h

        def side_to_core(xo):
            return send(win.at[side_p, xo, side, rows], win.at[3 - 2 * core, xo, side, rows], other_core)

        over_x[2].wait_recv()
        xo = from_xs[2]
        hops = [
            send(win.at[2, xo, hi, rows], win.at[0, xo, hi, rows], next_),
            send(win.at[2, xo, hi, rows], win.at[4, xo, hi, rows], prev),
        ]
        copies = []
        for j in (2, 0, 1):
            if j != 2:
                over_x[j].wait_recv()
            copies.append(
                send(
                    win.at[2, from_xs[j], hi, rows], win.at[1 + 2 * core, from_xs[j], hi, rows], other_core
                )
            )
        for j in range(2):
            over_prev[j].wait_recv()
            over_next[j].wait_recv()
            copies.append(side_to_core(from_xs[j]))
        for copy in hops:
            copy.wait_recv()
        copies.append(side_to_core(xo))
        return copies

    def sides(flip):
        parts = [h_prev, jnp.where(core == 0, h_prev, h), h, jnp.where(core == 0, h, h_next), h_next]
        return parts if flip == 0 else [1 - part for part in parts]

    to_far = [send(win.at[2, x, h, rows], win.at[2, x, h, rows], far) for rows in tiles]
    to_next, to_prev, over_x, to_core = spread(0, shard)

    load_slots.wait()

    @pl.loop(0, SHARDS)
    def _(s):
        for t in range(2):
            for d in range(2):
                index = d * (slots + 1) + jnp.clip(slot_of[8 * d, 2 * s + t], 0, slots)
                adj[s, pl.ds(d * TILE, TILE), pl.ds(t * TILE, TILE)] = mask_rows[index]
                adj_t[s, pl.ds(t * TILE, TILE), pl.ds(d * TILE, TILE)] = mask_cols[index]

    over_prev, over_next, side_core = spread_sides(0, shard, to_next, to_prev)
    cores_0 = spread_cores(0, shard, over_x, over_prev, over_next)

    summed[...] = jnp.zeros((SHARD, TILE), F32)

    def aggregate(blocks, parts):
        total = summed[...]
        for p in blocks:
            for xo in range(XS):
                total = total + jnp.dot(
                    adj[(p * XS + xo) * 2 + parts[p]], win[p, xo, parts[p]], preferred_element_type=F32
                )
        summed[...] = total

    parts_0, parts_1 = sides(0), sides(1)
    aggregate((0, 2, 4), parts_0)

    to_core.wait_recv()
    side_core.wait_recv()
    for copy in cores_0:
        copy.wait_recv()
    aggregate((1, 3), parts_0)

    to_far[0].wait_recv()
    to_next_0, to_prev_0, over_x_0, to_core_0 = spread(1, tiles[0])
    over_prev_0, over_next_0, side_core_0 = spread_sides(1, tiles[0], to_next_0, to_prev_0)
    to_far[1].wait_recv()
    to_next_1, to_prev_1, over_x_1, to_core_1 = spread(1, tiles[1])
    cores_1 = spread_cores(1, tiles[0], over_x_0, over_prev_0, over_next_0)
    over_prev_1, over_next_1, side_core_1 = spread_sides(1, tiles[1], to_next_1, to_prev_1)
    cores_1 += spread_cores(1, tiles[1], over_x_1, over_prev_1, over_next_1)
    aggregate((0, 2, 4), parts_1)
    for copy in (to_core_0, side_core_0, to_core_1, side_core_1, *cores_1):
        copy.wait_recv()
    aggregate((1, 3), parts_1)

    load_neigh.wait()
    load_cotangent.wait()
    scaling = 1.0 / (1.0 + degree[...])
    mean_rows[...] = (summed[...] * scaling).astype(BF16)
    preact = pre_self[...] + jnp.dot(mean_rows[...], w_neigh[...], preferred_element_type=F32)
    sigmoid = jax.nn.sigmoid(preact)
    output[...] = (preact * sigmoid).astype(BF16)
    grad_pre = (cotangent[...].astype(F32) * sigmoid * (1.0 + preact * (1.0 - sigmoid))).astype(BF16)
    rows_first = (((0,), (0,)), ((), ()))
    hidden_last = (((1,), (1,)), ((), ()))
    grads[0] = lax.dot_general(win[2, x, h], grad_pre, rows_first, preferred_element_type=F32)
    grads[1] = lax.dot_general(mean_rows[...], grad_pre, rows_first, preferred_element_type=F32)
    core_grads = send(grads.at[1 - core], grads_core, other_core)
    pulled[...] = (
        lax.dot_general(grad_pre, w_neigh[...], hidden_last, preferred_element_type=F32) * scaling
    ).astype(BF16)
    local_term[...] = lax.dot_general(grad_pre, w_self[...], hidden_last, preferred_element_type=F32)

    def term(p, xo, part, rows):
        return jnp.dot(adj_t[(p * XS + xo) * 2 + part, rows, :], pulled[...], preferred_element_type=F32)

    class Back:
        def __init__(self, phase, rows):
            self.phase, self.rows = phase, rows
            self.parts = parts_1 if phase else parts_0

        def core_sum(self, q, xo):
            return term(2 * q, xo, self.parts[2 * q], self.rows) + core_in[self.phase, q, xo, self.rows].astype(F32)

        def to_cores(self):
            self.cores = []
            for i in range(2):
                p = 2 * i + 1
                for xo in range(XS):
                    core_out[self.phase, i, xo, self.rows] = term(p, xo, self.parts[p], self.rows).astype(BF16)
                source = core_out.at[self.phase, i, :, self.rows]
                target = core_in.at[self.phase, i + core, :, self.rows]
                self.cores.append(send(source, target, other_core))

        def over(self):
            for copy in self.cores:
                copy.wait_recv()
            self.hops = []
            for i, device in enumerate((prev, next_)):
                zx_out[self.phase, i, self.rows] = self.core_sum(2 * i, xs[2]).astype(BF16)
                target = zx_in.at[self.phase, 1 - i, self.rows]
                self.hops.append(send(zx_out.at[self.phase, i, self.rows], target, device))
            self.x = {}
            for q in (0, 2, 1):
                for j in range(2):
                    self.to_x(q, j, self.core_sum(q, xs[j]))
            for q in range(3):
                own_part[self.phase, q, self.rows] = self.core_sum(q, x)

        def to_x(self, q, j, value):
            x_out[self.phase, q, j, self.rows] = value.astype(BF16)
            source, target = x_out.at[self.phase, q, j, self.rows], x_in.at[self.phase, q, j, self.rows]
            self.x[q, j] = send(source, target, x_devices[j])

        def over_two(self):
            for copy in self.hops:
                copy.wait_recv()
            value = self.core_sum(1, xs[2])
            for i in range(2):
                value = value + zx_in[self.phase, i, self.rows].astype(F32)
            self.to_x(1, 2, value)

        def x_sum(self, q, count):
            total = own_part[self.phase, q, self.rows]
            for j in range(count):
                self.x[q, j].wait_recv()
                total = total + x_in[self.phase, q, j, self.rows].astype(F32)
            return total

        def to_sides(self):
            self.sides = []
            for i, device in enumerate((prev, next_)):
                z_out[self.phase, i, self.rows] = self.x_sum(2 * i, 2).astype(BF16)
                target = z_in.at[self.phase, 1 - i, self.rows]
                self.sides.append(send(z_out.at[self.phase, i, self.rows], target, device))

        def total(self):
            total = self.x_sum(1, 3)
            for copy in self.sides:
                copy.wait_recv()
            for i in range(2):
                total = total + z_in[self.phase, i, self.rows].astype(F32)
            return total

        def to_far(self):
            far_out[self.rows] = self.total().astype(BF16)
            return send(far_out.at[self.rows], far_in.at[self.rows], far)

    first, second, near = Back(1, tiles[0]), Back(1, tiles[1]), Back(0, shard)
    piece_rows = TILE // PLANE
    own_rows = pl.ds(place * piece_rows, piece_rows)

    first.to_cores()
    core_grads.wait_recv()
    grads[core] = grads[core] + grads_core[...]
    plane_grads = [
        send(grads.at[core, pl.ds(to * piece_rows, piece_rows)], grads_plane.at[i], device)
        for i, (to, device) in enumerate(zip(places, plane_devices, strict=True))
    ]
    second.to_cores()
    first.over()
    for copy in plane_grads:
        copy.wait_recv()
    part = grads[core, own_rows]
    for i in range(PLANE - 1):
        part = part + grads_plane[i]
    grads_near[near_slot] = part
    near_grads = [send(grads_near.at[near_slot], grads_near.at[near_slot], device) for device in near_devices]
    second.over()
    first.over_two()
    for copy in near_grads:
        copy.wait_recv()
    part = grads_near[0]
    for i in range(1, NEAR):
        part = part + grads_near[i]
    grads_far[far_slot] = part
    far_grads = [send(grads_far.at[far_slot], grads_far.at[far_slot], device) for device in far_devices]
    second.over_two()
    first.to_sides()
    near.to_cores()
    far_back = [first.to_far()]
    second.to_sides()
    far_back.append(second.to_far())
    near.over()
    near.over_two()
    for copy in far_grads:
        copy.wait_recv()
    factor = 1.0 / math.sqrt(SHARD * lax.axis_size("wide") * lax.axis_size("narrow"))
    piece = grads_all.at[core, own_rows]
    piece[...] = (grads_far[0] + grads_far[1] + grads_far[2] + grads_far[3]) * factor
    plane_grads = [send(piece, piece, device) for device in plane_devices]
    near.to_sides()
    for copy in plane_grads:
        copy.wait_recv()
    core_grads = send(grads_all.at[core], grads_all.at[core], other_core)
    own_total[...] = local_term[...] + near.total()
    for t in range(2):
        far_back[t].wait_recv()
        grad_input[tiles[t]] = (own_total[tiles[t]] + far_in[tiles[t]].astype(F32)).astype(BF16)
    core_grads.wait_recv()
    grad_self[...] = grads_all[0]
    grad_neigh[...] = grads_all[1]
    for copy in sent:
        copy.wait_send()


def body(features, w_self, w_neigh, cotangent, tile_src, tile_live, tile_mask):
    rows, width = features.shape
    hidden = w_self.shape[1]
    slots = tile_src.shape[1]
    vmem = pl.BlockSpec(memory_space=pltpu.VMEM)
    hbm = pl.BlockSpec(memory_space=pl.ANY)
    return pl.pallas_call(
        functools.partial(kernel, slots),
        out_shape=(
            jax.ShapeDtypeStruct((rows, hidden), BF16),
            jax.ShapeDtypeStruct((width, hidden), F32),
            jax.ShapeDtypeStruct((width, hidden), F32),
            jax.ShapeDtypeStruct((rows, width), BF16),
        ),
        in_specs=[hbm] * 7,
        out_specs=[vmem] * 4,
        scratch_shapes=[
            pltpu.VMEM((width, hidden), BF16),
            pltpu.VMEM((width, hidden), BF16),
            pltpu.VMEM((rows, hidden), BF16),
            pltpu.SMEM(tile_src.shape, jnp.int32),
            pltpu.SMEM(tile_live.shape, jnp.int32),
            pltpu.VMEM((2, slots, TILE, TILE), jnp.int32),
            pltpu.VMEM((2 * (slots + 1), TILE, TILE), BF16),
            pltpu.VMEM((2 * (slots + 1), TILE, TILE), BF16),
            pltpu.VMEM((16, TILE), jnp.int32),
            pltpu.SMEM((16, TILE), jnp.int32),
            pltpu.VMEM((SHARDS, SHARD, SHARD), BF16),
            pltpu.VMEM((SHARDS, SHARD, SHARD), BF16),
            pltpu.VMEM((WINDOW, XS, 2, SHARD, TILE), BF16),
            pltpu.VMEM((SHARD, TILE), F32),
            pltpu.VMEM((SHARD, TILE), F32),
            pltpu.VMEM((SHARD, hidden), F32),
            pltpu.VMEM((SHARD, TILE), BF16),
            pltpu.VMEM((SHARD, TILE), BF16),
            pltpu.VMEM((SHARD, TILE), F32),
            pltpu.VMEM((2, 2, XS, SHARD, TILE), BF16),
            pltpu.VMEM((2, 3, XS, SHARD, TILE), BF16),
            pltpu.VMEM((2, 3, 3, SHARD, TILE), BF16),
            pltpu.VMEM((2, 3, 3, SHARD, TILE), BF16),
            pltpu.VMEM((2, 3, SHARD, TILE), F32),
            pltpu.VMEM((2, 2, SHARD, TILE), BF16),
            pltpu.VMEM((2, 2, SHARD, TILE), BF16),
            pltpu.VMEM((2, 2, SHARD, TILE), BF16),
            pltpu.VMEM((2, 2, SHARD, TILE), BF16),
            pltpu.VMEM((SHARD, TILE), F32),
            pltpu.VMEM((SHARD, TILE), BF16),
            pltpu.VMEM((SHARD, TILE), BF16),
            pltpu.VMEM((2, width, hidden), F32),
            pltpu.VMEM((width, hidden), F32),
            pltpu.VMEM((PLANE - 1, width // PLANE, hidden), F32),
            pltpu.VMEM((NEAR, width // PLANE, hidden), F32),
            pltpu.VMEM((FAR, width // PLANE, hidden), F32),
            pltpu.VMEM((2, width, hidden), F32),
            pltpu.SemaphoreType.DMA((TRANSFERS,)),
            pltpu.SemaphoreType.DMA((TRANSFERS,)),
            pltpu.SemaphoreType.DMA((7,)),
            pltpu.SemaphoreType.DMA,
        ],
        compiler_params=pltpu.CompilerParams(
            collective_id=1, has_side_effects=True, vmem_limit_bytes=62 * 1024 * 1024
        ),
    )(features, w_self, w_neigh, cotangent, tile_src, tile_live, tile_mask)


def solution(mesh):
    return jax.shard_map(
        body,
        mesh=mesh,
        in_specs=(
            P(("wide", "narrow"), None),
            P(),
            P(),
            P(("wide", "narrow"), None),
            P(("wide", "narrow"), None),
            P(("wide", "narrow")),
            P(("wide", "narrow"), None, None, None),
        ),
        out_specs=(P(("wide", "narrow"), None), P(), P(), P(("wide", "narrow"), None)),
        check_vma=False,
    )
```

```python
import functools
import math

import jax
import jax.numpy as jnp
from jax import lax
from jax.experimental import pallas as pl
from jax.experimental.pallas import tpu as pltpu
from jax.sharding import PartitionSpec as P

REACH = 2
WINDOW = 2 * REACH + 1
XS, YS, ZS, CORES = 4, 4, 32, 2
Z_LO = 16
TILE = 128
SHARD = 2 * TILE
BLOCK_TILES = 16
WINDOW_TILES = WINDOW * BLOCK_TILES
SHARDS = WINDOW_TILES // 2
PLANE = XS * YS
NEAR, FAR = 8, 4
TRANSFERS = 192
F32 = jnp.float32
BF16 = jnp.bfloat16


def device_of(x, y, z, core):
    return ((y * Z_LO + z % Z_LO) * CORES + core, x * 2 + z // Z_LO)


def kernel(
    slots,
    features_hbm,
    w_self_hbm,
    w_neigh_hbm,
    cotangent_hbm,
    tile_src_hbm,
    tile_live_hbm,
    tile_mask_hbm,
    output,
    grad_self,
    grad_neigh,
    grad_input,
    w_self,
    w_neigh,
    cotangent,
    tile_src,
    tile_live,
    mask_in,
    mask_rows,
    mask_cols,
    slot_vec,
    slot_of,
    adj,
    adj_t,
    win,
    summed,
    degree,
    pre_self,
    mean_rows,
    pulled,
    local_term,
    core_out,
    core_in,
    x_out,
    x_in,
    own_part,
    zx_out,
    zx_in,
    z_out,
    z_in,
    own_total,
    far_out,
    far_in,
    grads,
    grads_core,
    grads_plane,
    grads_near,
    grads_far,
    grads_all,
    send_sem,
    recv_sem,
    load_sem,
    slot_sem,
):
    wide, narrow = lax.axis_index("wide"), lax.axis_index("narrow")
    core = wide % 2
    z_lo = (wide // 2) % Z_LO
    y = wide // (2 * Z_LO)
    x = narrow // 2
    h = narrow % 2
    z = h * Z_LO + z_lo

    other_core = device_of(x, y, z, 1 - core)
    xs = [(x + step) % XS for step in (1, 3, 2)]
    from_xs = [xs[1], xs[0], xs[2]]
    x_devices = [device_of(to, y, z, core) for to in xs]
    far = device_of(x, y, (z + 16) % ZS, core)
    prev_y = jnp.where(z_lo == 0, (y + YS - 1) % YS, y)
    next_y = jnp.where(z_lo == Z_LO - 1, (y + 1) % YS, y)
    prev_z, next_z = (z + ZS - 1) % ZS, (z + 1) % ZS
    prev = device_of(x, prev_y, prev_z, core)
    next_ = device_of(x, next_y, next_z, core)
    place = y * XS + x
    places = [(place + step) % PLANE for step in range(1, PLANE)]
    plane_devices = [device_of(to % XS, to // XS, z, core) for to in places]
    near_slot, far_slot = z % NEAR, z // NEAR
    near_devices = [
        device_of(x, y, far_slot * NEAR + (near_slot + step) % NEAR, core) for step in range(1, NEAR)
    ]
    far_devices = [
        device_of(x, y, ((far_slot + step) % FAR) * NEAR + near_slot, core) for step in range(1, FAR)
    ]
    h_prev, h_next = prev_z // Z_LO, next_z // Z_LO

    barrier = pltpu.get_barrier_semaphore()
    greeted = [other_core, *plane_devices, prev, next_, *near_devices, *far_devices]
    for device in greeted:
        pl.semaphore_signal(barrier, inc=1, device_id=device, device_id_type=pl.DeviceIdType.MESH)

    sent = []

    def send(source, target, device):
        number = len(sent)
        copy = pltpu.make_async_remote_copy(
            src_ref=source,
            dst_ref=target,
            send_sem=send_sem.at[number],
            recv_sem=recv_sem.at[number],
            device_id=device,
            device_id_type=pl.DeviceIdType.MESH,
        )
        copy.start()
        sent.append(copy)
        return copy

    loads = [
        pltpu.make_async_copy(source, target, load_sem.at[number])
        for number, (source, target) in enumerate(
            (
                (tile_src_hbm, tile_src),
                (tile_live_hbm, tile_live),
                (features_hbm, win.at[2, x, h]),
                (w_self_hbm, w_self),
                (tile_mask_hbm, mask_in),
                (w_neigh_hbm, w_neigh),
                (cotangent_hbm, cotangent),
            )
        )
    ]
    for load in loads:
        load.start()
    load_src, load_live, load_features, load_self, load_mask, load_neigh, load_cotangent = loads

    load_src.wait()
    load_live.wait()
    window_tile = lax.broadcasted_iota(jnp.int32, (8, TILE), 1)
    for d in range(2):

        def find(c, found, d=d):
            source = jnp.where(c < tile_live[d], tile_src[d, c], -1)
            return jnp.where(window_tile == source, c, found)

        slot_vec[d * 8 : d * 8 + 8, :] = lax.fori_loop(0, slots, find, jnp.full((8, TILE), slots, jnp.int32))
    load_slots = pltpu.make_async_copy(slot_vec, slot_of, slot_sem)
    load_slots.start()

    load_features.wait()
    load_self.wait()
    pre_self[...] = jnp.dot(win[2, x, h], w_self[...], preferred_element_type=F32)
    core_in[0, 2 * core] = jnp.zeros((XS, SHARD, TILE), BF16)
    core_in[1, 2 * core] = jnp.zeros((XS, SHARD, TILE), BF16)
    for d in range(2):
        mask_rows[d * (slots + 1) + slots] = jnp.zeros((TILE, TILE), BF16)
        mask_cols[d * (slots + 1) + slots] = jnp.zeros((TILE, TILE), BF16)

    load_mask.wait()
    degree[...] = jnp.zeros((SHARD, TILE), F32)
    for d in range(2):

        @pl.loop(0, slots)
        def _(c, d=d):
            used = jnp.where(c < tile_live[d], 1, 0)
            degree[pl.ds(d * TILE, TILE)] += (mask_in[d, c] * used).astype(F32)
            tile = mask_in[d, c].astype(F32)
            mask_rows[d * (slots + 1) + c] = tile.astype(BF16)
            mask_cols[d * (slots + 1) + c] = tile.T.astype(BF16)

    degree[...] = jnp.dot(degree[...].astype(BF16), jnp.ones((TILE, TILE), BF16), preferred_element_type=F32)

    pl.semaphore_wait(barrier, len(greeted))

    side_p = 4 - 4 * core
    side_h = jnp.where(core == 0, h_next, h_prev)
    shard = pl.ds(0, SHARD)
    tiles = [pl.ds(t * TILE, TILE) for t in range(2)]

    def spread(flip, rows):
        hi = h if flip == 0 else 1 - h
        own = win.at[2, x, hi, rows]
        to_next = send(own, win.at[0, x, hi, rows], next_)
        to_prev = send(own, win.at[4, x, hi, rows], prev)
        over_x = [send(own, own, x_devices[j]) for j in (2, 0, 1)]
        over_x = [over_x[1], over_x[2], over_x[0]]
        to_core = send(own, win.at[1 + 2 * core, x, hi, rows], other_core)
        return to_next, to_prev, over_x, to_core

    def spread_sides(flip, rows, to_next, to_prev):
        hi_prev, hi_next = (h_prev, h_next) if flip == 0 else (1 - h_prev, 1 - h_next)
        side = side_h if flip == 0 else 1 - side_h
        to_next.wait_recv()
        from_prev = win.at[0, x, hi_prev, rows]
        over_prev = [send(from_prev, from_prev, device) for device in x_devices[:2]]
        to_prev.wait_recv()
        from_next = win.at[4, x, hi_next, rows]
        over_next = [send(from_next, from_next, device) for device in x_devices[:2]]
        to_core = send(win.at[side_p, x, side, rows], win.at[3 - 2 * core, x, side, rows], other_core)
        return over_prev, over_next, to_core

    def spread_cores(flip, rows, over_x, over_prev, over_next):
        hi = h if flip == 0 else 1 - h
        side = side_h if flip == 0 else 1 - side_h

        def side_to_core(xo):
            return send(win.at[side_p, xo, side, rows], win.at[3 - 2 * core, xo, side, rows], other_core)

        over_x[2].wait_recv()
        xo = from_xs[2]
        hops = [
            send(win.at[2, xo, hi, rows], win.at[0, xo, hi, rows], next_),
            send(win.at[2, xo, hi, rows], win.at[4, xo, hi, rows], prev),
        ]
        copies = []
        for j in (2, 0, 1):
            if j != 2:
                over_x[j].wait_recv()
            copies.append(
                send(
                    win.at[2, from_xs[j], hi, rows], win.at[1 + 2 * core, from_xs[j], hi, rows], other_core
                )
            )
        for j in range(2):
            over_prev[j].wait_recv()
            over_next[j].wait_recv()
            copies.append(side_to_core(from_xs[j]))
        for copy in hops:
            copy.wait_recv()
        copies.append(side_to_core(xo))
        return copies

    def sides(flip):
        parts = [h_prev, jnp.where(core == 0, h_prev, h), h, jnp.where(core == 0, h, h_next), h_next]
        return parts if flip == 0 else [1 - part for part in parts]

    to_far = [send(win.at[2, x, h, rows], win.at[2, x, h, rows], far) for rows in tiles]
    to_next, to_prev, over_x, to_core = spread(0, shard)

    load_slots.wait()

    @pl.loop(0, SHARDS)
    def _(s):
        for t in range(2):
            for d in range(2):
                index = d * (slots + 1) + jnp.clip(slot_of[8 * d, 2 * s + t], 0, slots)
                adj[s, pl.ds(d * TILE, TILE), pl.ds(t * TILE, TILE)] = mask_rows[index]
                adj_t[s, pl.ds(t * TILE, TILE), pl.ds(d * TILE, TILE)] = mask_cols[index]

    over_prev, over_next, side_core = spread_sides(0, shard, to_next, to_prev)
    cores_0 = spread_cores(0, shard, over_x, over_prev, over_next)

    summed[...] = jnp.zeros((SHARD, TILE), F32)

    def aggregate(blocks, parts):
        total = summed[...]
        for p in blocks:
            for xo in range(XS):
                total = total + jnp.dot(
                    adj[(p * XS + xo) * 2 + parts[p]], win[p, xo, parts[p]], preferred_element_type=F32
                )
        summed[...] = total

    parts_0, parts_1 = sides(0), sides(1)
    aggregate((0, 2, 4), parts_0)

    to_far[0].wait_recv()
    to_next_0, to_prev_0, over_x_0, to_core_0 = spread(1, tiles[0])
    to_core.wait_recv()
    side_core.wait_recv()
    for copy in cores_0:
        copy.wait_recv()
    aggregate((1, 3), parts_0)
    over_prev_0, over_next_0, side_core_0 = spread_sides(1, tiles[0], to_next_0, to_prev_0)
    to_far[1].wait_recv()
    to_next_1, to_prev_1, over_x_1, to_core_1 = spread(1, tiles[1])
    cores_1 = spread_cores(1, tiles[0], over_x_0, over_prev_0, over_next_0)
    over_prev_1, over_next_1, side_core_1 = spread_sides(1, tiles[1], to_next_1, to_prev_1)
    cores_1 += spread_cores(1, tiles[1], over_x_1, over_prev_1, over_next_1)
    aggregate((0, 2, 4), parts_1)
    for copy in (to_core_0, side_core_0, to_core_1, side_core_1, *cores_1):
        copy.wait_recv()
    aggregate((1, 3), parts_1)

    load_neigh.wait()
    load_cotangent.wait()
    scaling = 1.0 / (1.0 + degree[...])
    mean_rows[...] = (summed[...] * scaling).astype(BF16)
    preact = pre_self[...] + jnp.dot(mean_rows[...], w_neigh[...], preferred_element_type=F32)
    sigmoid = jax.nn.sigmoid(preact)
    grad_pre = (cotangent[...].astype(F32) * sigmoid * (1.0 + preact * (1.0 - sigmoid))).astype(BF16)
    rows_first = (((0,), (0,)), ((), ()))
    hidden_last = (((1,), (1,)), ((), ()))
    grads[0] = lax.dot_general(win[2, x, h], grad_pre, rows_first, preferred_element_type=F32)
    grads[1] = lax.dot_general(mean_rows[...], grad_pre, rows_first, preferred_element_type=F32)
    core_grads = send(grads.at[1 - core], grads_core, other_core)
    pulled[...] = (
        lax.dot_general(grad_pre, w_neigh[...], hidden_last, preferred_element_type=F32) * scaling
    ).astype(BF16)

    def term(p, xo, part, rows):
        return jnp.dot(adj_t[(p * XS + xo) * 2 + part, rows, :], pulled[...], preferred_element_type=F32)

    class Back:
        def __init__(self, phase, rows):
            self.phase, self.rows = phase, rows
            self.parts = parts_1 if phase else parts_0

        def core_sum(self, q, xo):
            return term(2 * q, xo, self.parts[2 * q], self.rows) + core_in[self.phase, q, xo, self.rows].astype(F32)

        def to_cores(self):
            self.cores = []
            for i in range(2):
                p = 2 * i + 1
                for xo in range(XS):
                    core_out[self.phase, i, xo, self.rows] = term(p, xo, self.parts[p], self.rows).astype(BF16)
                source = core_out.at[self.phase, i, :, self.rows]
                target = core_in.at[self.phase, i + core, :, self.rows]
                self.cores.append(send(source, target, other_core))

        def over(self):
            for copy in self.cores:
                copy.wait_recv()
            self.hops = []
            for i, device in enumerate((prev, next_)):
                zx_out[self.phase, i, self.rows] = self.core_sum(2 * i, xs[2]).astype(BF16)
                target = zx_in.at[self.phase, 1 - i, self.rows]
                self.hops.append(send(zx_out.at[self.phase, i, self.rows], target, device))
            self.x = {}
            for q in (0, 2, 1):
                for j in range(2):
                    self.to_x(q, j, self.core_sum(q, xs[j]))
            for q in range(3):
                own_part[self.phase, q, self.rows] = self.core_sum(q, x)

        def to_x(self, q, j, value):
            x_out[self.phase, q, j, self.rows] = value.astype(BF16)
            source, target = x_out.at[self.phase, q, j, self.rows], x_in.at[self.phase, q, j, self.rows]
            self.x[q, j] = send(source, target, x_devices[j])

        def over_two(self):
            for copy in self.hops:
                copy.wait_recv()
            value = self.core_sum(1, xs[2])
            for i in range(2):
                value = value + zx_in[self.phase, i, self.rows].astype(F32)
            self.to_x(1, 2, value)

        def x_sum(self, q, count):
            total = own_part[self.phase, q, self.rows]
            for j in range(count):
                self.x[q, j].wait_recv()
                total = total + x_in[self.phase, q, j, self.rows].astype(F32)
            return total

        def to_sides(self):
            self.sides = []
            for i, device in enumerate((prev, next_)):
                z_out[self.phase, i, self.rows] = self.x_sum(2 * i, 2).astype(BF16)
                target = z_in.at[self.phase, 1 - i, self.rows]
                self.sides.append(send(z_out.at[self.phase, i, self.rows], target, device))

        def total(self):
            total = self.x_sum(1, 3)
            for copy in self.sides:
                copy.wait_recv()
            for i in range(2):
                total = total + z_in[self.phase, i, self.rows].astype(F32)
            return total

        def to_far(self):
            far_out[self.rows] = self.total().astype(BF16)
            return send(far_out.at[self.rows], far_in.at[self.rows], far)

    first, second, near = Back(1, tiles[0]), Back(1, tiles[1]), Back(0, shard)
    piece_rows = TILE // PLANE
    own_rows = pl.ds(place * piece_rows, piece_rows)

    first.to_cores()
    core_grads.wait_recv()
    grads[core] = grads[core] + grads_core[...]
    plane_grads = [
        send(grads.at[core, pl.ds(to * piece_rows, piece_rows)], grads_plane.at[i], device)
        for i, (to, device) in enumerate(zip(places, plane_devices, strict=True))
    ]
    second.to_cores()
    output[...] = (preact * sigmoid).astype(BF16)
    local_term[...] = lax.dot_general(grad_pre, w_self[...], hidden_last, preferred_element_type=F32)
    first.over()
    for copy in plane_grads:
        copy.wait_recv()
    part = grads[core, own_rows]
    for i in range(PLANE - 1):
        part = part + grads_plane[i]
    grads_near[near_slot] = part
    near_grads = [send(grads_near.at[near_slot], grads_near.at[near_slot], device) for device in near_devices]
    second.over()
    first.over_two()
    for copy in near_grads:
        copy.wait_recv()
    part = grads_near[0]
    for i in range(1, NEAR):
        part = part + grads_near[i]
    grads_far[far_slot] = part
    far_grads = [send(grads_far.at[far_slot], grads_far.at[far_slot], device) for device in far_devices]
    second.over_two()
    first.to_sides()
    near.to_cores()
    far_back = [first.to_far()]
    second.to_sides()
    far_back.append(second.to_far())
    near.over()
    near.over_two()
    for copy in far_grads:
        copy.wait_recv()
    factor = 1.0 / math.sqrt(SHARD * lax.axis_size("wide") * lax.axis_size("narrow"))
    piece = grads_all.at[core, own_rows]
    piece[...] = (grads_far[0] + grads_far[1] + grads_far[2] + grads_far[3]) * factor
    plane_grads = [send(piece, piece, device) for device in plane_devices]
    near.to_sides()
    for copy in plane_grads:
        copy.wait_recv()
    core_grads = send(grads_all.at[core], grads_all.at[core], other_core)
    own_total[...] = local_term[...] + near.total()
    for t in range(2):
        far_back[t].wait_recv()
        grad_input[tiles[t]] = (own_total[tiles[t]] + far_in[tiles[t]].astype(F32)).astype(BF16)
    core_grads.wait_recv()
    grad_self[...] = grads_all[0]
    grad_neigh[...] = grads_all[1]
    for copy in sent:
        copy.wait_send()


def body(features, w_self, w_neigh, cotangent, tile_src, tile_live, tile_mask):
    rows, width = features.shape
    hidden = w_self.shape[1]
    slots = tile_src.shape[1]
    vmem = pl.BlockSpec(memory_space=pltpu.VMEM)
    hbm = pl.BlockSpec(memory_space=pl.ANY)
    return pl.pallas_call(
        functools.partial(kernel, slots),
        out_shape=(
            jax.ShapeDtypeStruct((rows, hidden), BF16),
            jax.ShapeDtypeStruct((width, hidden), F32),
            jax.ShapeDtypeStruct((width, hidden), F32),
            jax.ShapeDtypeStruct((rows, width), BF16),
        ),
        in_specs=[hbm] * 7,
        out_specs=[vmem] * 4,
        scratch_shapes=[
            pltpu.VMEM((width, hidden), BF16),
            pltpu.VMEM((width, hidden), BF16),
            pltpu.VMEM((rows, hidden), BF16),
            pltpu.SMEM(tile_src.shape, jnp.int32),
            pltpu.SMEM(tile_live.shape, jnp.int32),
            pltpu.VMEM((2, slots, TILE, TILE), jnp.int32),
            pltpu.VMEM((2 * (slots + 1), TILE, TILE), BF16),
            pltpu.VMEM((2 * (slots + 1), TILE, TILE), BF16),
            pltpu.VMEM((16, TILE), jnp.int32),
            pltpu.SMEM((16, TILE), jnp.int32),
            pltpu.VMEM((SHARDS, SHARD, SHARD), BF16),
            pltpu.VMEM((SHARDS, SHARD, SHARD), BF16),
            pltpu.VMEM((WINDOW, XS, 2, SHARD, TILE), BF16),
            pltpu.VMEM((SHARD, TILE), F32),
            pltpu.VMEM((SHARD, TILE), F32),
            pltpu.VMEM((SHARD, hidden), F32),
            pltpu.VMEM((SHARD, TILE), BF16),
            pltpu.VMEM((SHARD, TILE), BF16),
            pltpu.VMEM((SHARD, TILE), F32),
            pltpu.VMEM((2, 2, XS, SHARD, TILE), BF16),
            pltpu.VMEM((2, 3, XS, SHARD, TILE), BF16),
            pltpu.VMEM((2, 3, 3, SHARD, TILE), BF16),
            pltpu.VMEM((2, 3, 3, SHARD, TILE), BF16),
            pltpu.VMEM((2, 3, SHARD, TILE), F32),
            pltpu.VMEM((2, 2, SHARD, TILE), BF16),
            pltpu.VMEM((2, 2, SHARD, TILE), BF16),
            pltpu.VMEM((2, 2, SHARD, TILE), BF16),
            pltpu.VMEM((2, 2, SHARD, TILE), BF16),
            pltpu.VMEM((SHARD, TILE), F32),
            pltpu.VMEM((SHARD, TILE), BF16),
            pltpu.VMEM((SHARD, TILE), BF16),
            pltpu.VMEM((2, width, hidden), F32),
            pltpu.VMEM((width, hidden), F32),
            pltpu.VMEM((PLANE - 1, width // PLANE, hidden), F32),
            pltpu.VMEM((NEAR, width // PLANE, hidden), F32),
            pltpu.VMEM((FAR, width // PLANE, hidden), F32),
            pltpu.VMEM((2, width, hidden), F32),
            pltpu.SemaphoreType.DMA((TRANSFERS,)),
            pltpu.SemaphoreType.DMA((TRANSFERS,)),
            pltpu.SemaphoreType.DMA((7,)),
            pltpu.SemaphoreType.DMA,
        ],
        compiler_params=pltpu.CompilerParams(
            collective_id=1, has_side_effects=True, vmem_limit_bytes=62 * 1024 * 1024
        ),
    )(features, w_self, w_neigh, cotangent, tile_src, tile_live, tile_mask)


def solution(mesh):
    return jax.shard_map(
        body,
        mesh=mesh,
        in_specs=(
            P(("wide", "narrow"), None),
            P(),
            P(),
            P(("wide", "narrow"), None),
            P(("wide", "narrow"), None),
            P(("wide", "narrow")),
            P(("wide", "narrow"), None, None, None),
        ),
        out_specs=(P(("wide", "narrow"), None), P(), P(), P(("wide", "narrow"), None)),
        check_vma=False,
    )
```
